512 devices in a mesh: dom: 128 (over z, y, core), sub: 4 (over x).
Axes of the slice: x: 4, y: 8, z: 8, core: 2. Of those that a mesh axis runs over, the one named last changes fastest.
Arguments:
- fine_nodes: float32 [524288, 128], P(('dom', 'sub')), may hold values from -6 to 6
- fine_edges: float32 [6, 524288, 128], P(None, ('dom', 'sub')), may hold values from -6 to 6
- fine_nbr: int32 [6, 524288], P(None, ('dom', 'sub')), may hold values from 0 to 1599, as said below
- sub_send: int32 [512, 4, 96], P(('dom', 'sub')), may hold values from 0 to 1023
- dom_send: int32 [512, 2, 96], P(('dom', 'sub')), may hold values from 0 to 1023
- pool_owner: int32 [524288, 1], P(('dom', 'sub')), may hold values from 0 to 127, as said below
- pool_slot: int32 [524288], P(('dom', 'sub')), may hold values from 0 to 255
- coarse_nbr: int32 [6, 131072], P(None, ('dom', 'sub')), may hold values from 0 to 383, as said below
- coarse_send: int32 [512, 2, 64], P(('dom', 'sub')), may hold values from 0 to 255
- fine_edge_in: float32 [384, 128], replicated, may hold values from -0.3125 to 0.3125
- fine_edge_out: float32 [128, 128], replicated, may hold values from -0.5 to 0.5
- fine_node_in: float32 [256, 128], replicated, may hold values from -0.375 to 0.375
- fine_node_out: float32 [128, 128], replicated, may hold values from -0.5 to 0.5
- coarse_edge_in: float32 [256, 128], replicated, may hold values from -0.375 to 0.375
- coarse_edge_out: float32 [128, 128], replicated, may hold values from -0.5 to 0.5
- coarse_node_in: float32 [256, 128], replicated, may hold values from -0.375 to 0.375
- coarse_node_out: float32 [128, 128], replicated, may hold values from -0.5 to 0.5
Outputs:
- fine_out: float32 [524288, 128], P(('dom', 'sub'))
The draws below stay inside these ranges and needn't reach their ends.
Inputs may be any that keep to these rules, and one draw needn't show every extreme that they name: `fine_nbr`: indexes the device's 1024 own rows, then 4 blocks of 96 rows from the siblings along sub in order, then 96 rows from the previous and 96 from the next device along dom. `sub_send`: local rows of the sending device. `dom_send`: slot 0 goes to the next device along dom, slot 1 to the previous; local rows of the sender. `pool_owner`: the owner is the device with this dom index and the same sub index; it is the row's own dom index or one next to it; among the rows of one device exactly 128 name the next dom index and exactly 128 the previous one where these exist, the others their own. `coarse_nbr`: indexes the device's 256 own coarse rows, then 64 rows from the previous and 64 from the next device along dom. `coarse_send`: slot 0 goes to the next device along dom, slot 1 to the previous; local coarse rows of the sender.
All inputs are finite; a program needn't handle non-finite values.
Results may differ from the reference program's by a relative error of at most 0.0003.
Values sent between devices are 32-bit elements; how exact they have to be, the bound alone decides.
No kernel may reach another device: no remote copies, remote signals or barrier semaphores. Data moves between devices by JAX's collectives and lax.ppermute only.
A program may use at most 64 MiB of HBM per device.

```python
import jax
import jax.numpy as jnp
from jax import lax

LATENT = 128
DEG = 6
CDEG = 6
NODE_DEV = 1024
HALO = 96
CHALO = 64
COARSE_DEV = 256
CAP = 128
EXT = 1600
CEXT = 384
FINE = 524288
COARSE = 131072
N_DOM = 128
N_SUB = 4
DEVICES = 512


def local_indices(key, rows, degree, own_count, total_count, far_in_twenty):
    first, second, third = jax.random.split(key, 3)
    own_pick = jax.random.randint(first, (degree, rows), 0, own_count)
    far_pick = jax.random.randint(second, (degree, rows), own_count, total_count)
    chooser = jax.random.randint(third, (degree, rows), 0, 20)
    result = jnp.where(chooser < far_in_twenty, far_pick, own_pick)
    result = result.at[0, 0].set(total_count - 1).at[1, 0].set(0)
    return result.astype(jnp.int32)


def draw_fine_nbr(key, part):
    key = jax.random.fold_in(key, 11)
    return local_indices(key, FINE, DEG, NODE_DEV, EXT, 3)


def draw_coarse_nbr(key, part):
    key = jax.random.fold_in(key, 23)
    return local_indices(key, COARSE, CDEG, COARSE_DEV, CEXT, 4)


def draw_pool_owner(key, part):
    key = jax.random.fold_in(key, 37)
    places = jnp.arange(NODE_DEV, dtype=jnp.int32)
    base_steps = jnp.where(places < CAP, -1, jnp.where(places < 2 * CAP, 1, 0)).astype(jnp.int32)
    device_keys = jax.random.split(key, DEVICES)
    orders = jax.vmap(lambda one_key: jax.random.permutation(one_key, NODE_DEV))(device_keys)
    steps_all = base_steps[orders]
    dom_index = (jnp.arange(DEVICES, dtype=jnp.int32) // N_SUB)[:, None]
    owners = jnp.clip(dom_index + steps_all, 0, N_DOM - 1)
    return owners.reshape(FINE, 1).astype(jnp.int32)


def plant(values, own_key, smallest, high):
    index_at = [jax.random.randint(jax.random.fold_in(own_key, axis), (), 0, length) for axis, length in enumerate(values.shape)]
    widest = values.shape.index(max(values.shape))
    next_to = index_at[:widest] + [(index_at[widest] + 1) % values.shape[widest]] + index_at[widest + 1:]
    return values.at[tuple(index_at)].set(smallest).at[tuple(next_to)].set(high)


def block_scale(own_key, shape, cuts, low, high):
    def one(dim, blocks):
        heights = jax.random.uniform(jax.random.fold_in(jax.random.fold_in(own_key, 6), dim), (blocks,), jnp.float32, low / len(cuts), high / len(cuts))
        return jnp.repeat(jnp.exp(heights), shape[dim] // blocks).reshape((-1,) + (1,) * (len(shape) - dim - 1))

    factor_of = one(*cuts[0])
    for cut in cuts[1:]:
        factor_of = factor_of * one(*cut)
    return factor_of


def scatter_about(stream_key, dims, deviation, reach, cuts=(), held_as=jnp.bfloat16):
    values = jax.random.normal(stream_key, dims, jnp.float32) * deviation
    if len(cuts) > 0:
        values = block_scale(stream_key, dims, cuts, -0.22, 0.18) * values
    return jnp.clip(values, min=-reach, max=reach).astype(held_as)


def setup_inputs(seed: int = 0) -> dict:
    key_list = jax.random.split(jax.random.key(seed), 18)
    fine_nodes = scatter_about(key_list[0], (FINE, LATENT), 1.0, 6.0, ((0, 512),), jnp.float32)
    fine_edges = scatter_about(key_list[1], (DEG, FINE, LATENT), 1.0, 6.0, ((1, 512),), jnp.float32)
    fine_nbr = draw_fine_nbr(jax.random.fold_in(key_list[17], 71), 0)
    sub_send = plant(jax.random.randint(key_list[3], (DEVICES, N_SUB, HALO), 0, NODE_DEV), jax.random.fold_in(key_list[3], 1), 0, NODE_DEV - 1).astype(jnp.int32)
    dom_send = plant(jax.random.randint(key_list[4], (DEVICES, 2, HALO), 0, NODE_DEV), jax.random.fold_in(key_list[4], 1), 0, NODE_DEV - 1).astype(jnp.int32)
    pool_owner = draw_pool_owner(jax.random.fold_in(key_list[17], 71), 0)
    pool_slot = plant(jax.random.randint(key_list[6], (FINE,), 0, COARSE_DEV), jax.random.fold_in(key_list[6], 1), 0, COARSE_DEV - 1).astype(jnp.int32)
    coarse_nbr = draw_coarse_nbr(jax.random.fold_in(key_list[17], 71), 0)
    coarse_send = plant(jax.random.randint(key_list[8], (DEVICES, 2, CHALO), 0, COARSE_DEV), jax.random.fold_in(key_list[8], 1), 0, COARSE_DEV - 1).astype(jnp.int32)
    fine_edge_in = scatter_about(key_list[9], (3 * LATENT, LATENT), (3 * LATENT) ** -0.5, 0.3125, (), jnp.float32)
    fine_edge_out = scatter_about(key_list[10], (LATENT, LATENT), LATENT ** -0.5, 0.5, (), jnp.float32)
    fine_node_in = scatter_about(key_list[11], (2 * LATENT, LATENT), (2 * LATENT) ** -0.5, 0.375, (), jnp.float32)
    fine_node_out = scatter_about(key_list[12], (LATENT, LATENT), LATENT ** -0.5, 0.5, (), jnp.float32)
    coarse_edge_in = scatter_about(key_list[13], (2 * LATENT, LATENT), (2 * LATENT) ** -0.5, 0.375, (), jnp.float32)
    coarse_edge_out = scatter_about(key_list[14], (LATENT, LATENT), LATENT ** -0.5, 0.5, (), jnp.float32)
    coarse_node_in = scatter_about(key_list[15], (2 * LATENT, LATENT), (2 * LATENT) ** -0.5, 0.375, (), jnp.float32)
    coarse_node_out = scatter_about(key_list[16], (LATENT, LATENT), LATENT ** -0.5, 0.5, (), jnp.float32)
    return {"fine_nodes": fine_nodes, "fine_edges": fine_edges, "fine_nbr": fine_nbr, "sub_send": sub_send, "dom_send": dom_send, "pool_owner": pool_owner, "pool_slot": pool_slot, "coarse_nbr": coarse_nbr, "coarse_send": coarse_send, "fine_edge_in": fine_edge_in, "fine_edge_out": fine_edge_out, "fine_node_in": fine_node_in, "fine_node_out": fine_node_out, "coarse_edge_in": coarse_edge_in, "coarse_edge_out": coarse_edge_out, "coarse_node_in": coarse_node_in, "coarse_node_out": coarse_node_out}


highest = lax.Precision.HIGHEST

def layer_norm(values):
    centre = lax.optimization_barrier(jnp.mean(values, axis=-1, keepdims=True))
    shifted = values - centre
    spread = lax.optimization_barrier(jnp.mean(shifted * shifted, axis=-1, keepdims=True))
    return shifted * lax.rsqrt(spread + 1e-05)

def perceptron(inputs, weight_in, weight_out):
    hidden = jax.nn.relu(jnp.dot(inputs, weight_in, precision=highest))
    return layer_norm(jnp.dot(hidden, weight_out, precision=highest))

def pick_rows(table, indices):
    return table[indices]

def reference(fine_nodes, fine_edges, fine_nbr, sub_send, dom_send, pool_owner, pool_slot, coarse_nbr, coarse_send, fine_edge_in, fine_edge_out, fine_node_in, fine_node_out, coarse_edge_in, coarse_edge_out, coarse_node_in, coarse_node_out):
    latent_all = fine_nodes.reshape(N_DOM, N_SUB, NODE_DEV, LATENT)
    edge_all = jnp.moveaxis(fine_edges.reshape(DEG, N_DOM, N_SUB, NODE_DEV, LATENT), 0, 3)
    nbr_all = jnp.moveaxis(fine_nbr.reshape(DEG, N_DOM, N_SUB, NODE_DEV), 0, 3)
    sub_lists = sub_send.reshape(N_DOM, N_SUB, N_SUB, HALO)
    dom_lists = dom_send.reshape(N_DOM, N_SUB, 2, HALO)

    def fine_layer(position):
        below = jnp.maximum(position - 1, 0)
        above = jnp.minimum(position + 1, N_DOM - 1)
        group = latent_all[position]
        from_sibling = jax.vmap(pick_rows)(group, sub_lists[position])
        from_sibling = jnp.swapaxes(from_sibling, 0, 1).reshape(N_SUB, N_SUB * HALO, LATENT)
        lower = jax.vmap(pick_rows)(latent_all[below], dom_lists[below, :, 0])
        lower = jnp.where(position > 0, lower, jnp.zeros_like(lower))
        upper = jax.vmap(pick_rows)(latent_all[above], dom_lists[above, :, 1])
        upper = jnp.where(position < N_DOM - 1, upper, jnp.zeros_like(upper))
        extended = jnp.concatenate([group, from_sibling, lower, upper], axis=1)
        neighbours = jax.vmap(pick_rows)(extended, nbr_all[position])
        receiver = jnp.broadcast_to(group[:, :, None, :], neighbours.shape)
        edge_here = edge_all[position]
        edge_new = edge_here + perceptron(jnp.concatenate([receiver, neighbours, edge_here], axis=-1), fine_edge_in, fine_edge_out)
        summed = lax.optimization_barrier(jnp.sum(edge_new, axis=2))
        return group + perceptron(jnp.concatenate([group, summed], axis=-1), fine_node_in, fine_node_out)
    updated = lax.map(fine_layer, jnp.arange(N_DOM, dtype=jnp.int32))
    sub_index = jnp.arange(N_SUB, dtype=jnp.int32)[None, :, None]
    owners = pool_owner.reshape(N_DOM, N_SUB, NODE_DEV)
    slots = pool_slot.reshape(N_DOM, N_SUB, NODE_DEV)
    target = ((owners * N_SUB + sub_index) * COARSE_DEV + slots).reshape(-1).astype(jnp.int32)
    flat = updated.reshape(-1, LATENT)
    sums = jax.ops.segment_sum(flat, target, num_segments=COARSE)
    counts = jax.ops.segment_sum(jnp.ones((FINE,), jnp.float32), target, num_segments=COARSE)
    pooled = sums / jnp.maximum(counts, 1.0)[:, None]
    coarse_all = pooled.reshape(N_DOM, N_SUB, COARSE_DEV, LATENT)
    cnbr_all = jnp.moveaxis(coarse_nbr.reshape(CDEG, N_DOM, N_SUB, COARSE_DEV), 0, 3)
    coarse_lists = coarse_send.reshape(N_DOM, N_SUB, 2, CHALO)

    def coarse_layer(position):
        below = jnp.maximum(position - 1, 0)
        above = jnp.minimum(position + 1, N_DOM - 1)
        group = coarse_all[position]
        lower = jax.vmap(pick_rows)(coarse_all[below], coarse_lists[below, :, 0])
        lower = jnp.where(position > 0, lower, jnp.zeros_like(lower))
        upper = jax.vmap(pick_rows)(coarse_all[above], coarse_lists[above, :, 1])
        upper = jnp.where(position < N_DOM - 1, upper, jnp.zeros_like(upper))
        extended = jnp.concatenate([group, lower, upper], axis=1)
        neighbours = jax.vmap(pick_rows)(extended, cnbr_all[position])
        receiver = jnp.broadcast_to(group[:, :, None, :], neighbours.shape)
        message = perceptron(jnp.concatenate([receiver, neighbours], axis=-1), coarse_edge_in, coarse_edge_out)
        summed = lax.optimization_barrier(jnp.sum(message, axis=2))
        return group + perceptron(jnp.concatenate([group, summed], axis=-1), coarse_node_in, coarse_node_out)
    refined = lax.map(coarse_layer, jnp.arange(N_DOM, dtype=jnp.int32)).reshape(-1, LATENT)
    return flat + refined[target]
```

```python
import functools

import jax
import jax.numpy as jnp
from jax import lax
from jax.experimental import pallas as pl
from jax.experimental.pallas import tpu as pltpu
from jax.sharding import PartitionSpec as P

F32 = jnp.float32
BF16 = jnp.bfloat16
LANES = 128
VMEM = pltpu.VMEM
SMEM = pltpu.SMEM


def split(values):
    high = values.astype(BF16)
    low = (values - high.astype(F32)).astype(BF16)
    return high, low


def wide(values):
    return jnp.concatenate(split(values), axis=1)


def square(weight):
    row = jnp.concatenate(split(weight), axis=1)
    return jnp.concatenate([row, row], axis=0)


def centred(weight):
    return weight - jnp.mean(weight, axis=1, keepdims=True)


def fold(product):
    return product[:, :LANES] + product[:, LANES:]


def matmul(rows, weight_square):
    return fold(jnp.dot(wide(rows), weight_square, preferred_element_type=F32))


def pick(one_hot, table_wide):
    return fold(jnp.dot(one_hot, table_wide, preferred_element_type=F32))


def scaled(shifted):
    spread = jnp.mean(shifted * shifted, axis=-1, keepdims=True)
    return shifted * lax.rsqrt(spread + 1e-05)


def one_hot(condition):
    return jnp.where(condition, 1.0, 0.0).astype(BF16)


def iota(shape, axis):
    return lax.broadcasted_iota(jnp.int32, shape, axis).astype(F32)


def is_even():
    return lax.rem(lax.axis_index("dom"), 2) == 0


def copy_rows(source, index_of, target, start, count, unroll=8):
    def body(step, carry):
        base = pl.multiple_of(step * unroll, unroll)
        for offset in range(unroll):
            target[pl.ds(start + base + offset, 1), :] = source[
                pl.ds(index_of(base + offset), 1), :
            ]
        return carry

    lax.fori_loop(0, count // unroll, body, 0)


def pack_kernel(
    sub_send, dom_send, owner, slot, nodes, sibling_out, core_out, chip_out, select_out
):
    halo = sub_send.shape[2]
    even = is_even()
    towards_core = jnp.where(even, 0, 1)
    for sibling in range(sub_send.shape[1]):
        copy_rows(
            nodes, lambda i: sub_send[0, sibling, i], sibling_out.at[sibling], 0, halo
        )
    copy_rows(nodes, lambda i: dom_send[0, towards_core, i], core_out, 0, halo)
    copy_rows(nodes, lambda i: dom_send[0, 1 - towards_core, i], chip_out, 0, halo)
    step = owner[...] - lax.axis_index("dom")
    core_step = jnp.where(even, 1, -1)
    upper = one_hot(iota((LANES, LANES), 0) <= iota((LANES, LANES), 1))
    ranks = []
    for direction in (core_step, -core_step):
        chosen = jnp.where(step == direction, 1.0, 0.0)
        inside = jnp.dot(chosen.astype(BF16), upper, preferred_element_type=F32)
        total = jnp.broadcast_to(jnp.sum(chosen, axis=1, keepdims=True), chosen.shape)
        before = jnp.zeros_like(total)
        rows = lax.broadcasted_iota(jnp.int32, total.shape, 0)
        running = total
        for shift in (1, 2, 4):
            moved = pltpu.roll(running, shift, 0)
            running = running + jnp.where(rows >= shift, moved, 0.0)
        before = running - total
        ranks.append((step == direction, inside + before - 1.0))
    own_slot = slot[...].astype(F32)
    count = 2 * LANES
    select = jnp.where(
        ranks[0][0],
        ranks[0][1] + count,
        jnp.where(ranks[1][0], ranks[1][1] + (count + LANES), own_slot),
    )
    select_out[...] = select
    sent = jnp.zeros((8, 2 * LANES), F32)
    for block in range(8):
        place = one_hot(iota((2 * LANES, LANES), 0) == select[block : block + 1] - count)
        slots = jnp.broadcast_to(own_slot[block : block + 1] + 1.0, (8, LANES)).astype(BF16)
        sent = sent + lax.dot_general(
            slots, place, (((1,), (1,)), ((), ())), preferred_element_type=F32
        )
    core_out[pl.ds(halo, 8), :] = sent[:, :LANES]
    chip_out[pl.ds(halo, 8), :] = sent[:, LANES:]


def before_kernel(
    edges, nodes, edge_in, select, coarse_nbr, coarse_send,
    pre_out, table_out, columns_out, weights, own_part, stage,
):
    step = pl.program_id(0)
    features = LANES

    @pl.when(step == 0)
    def _():
        weights[...] = square(edge_in[2 * features :, :])
        node_rows = wide(nodes[...])
        own_part[...] = fold(
            jnp.dot(node_rows, square(edge_in[:features, :]), preferred_element_type=F32)
        )
        table_out[...] = fold(
            jnp.dot(
                node_rows, square(edge_in[features : 2 * features, :]), preferred_element_type=F32
            )
        )
        stage[...] = jnp.zeros_like(stage)
        stage[0:8, :] = select[...]
        stage[8:14, :] = coarse_nbr[:, :LANES].astype(F32)
        stage[16:22, :] = coarse_nbr[:, LANES:].astype(F32)
        stage[24:26, 0 : coarse_send.shape[2]] = coarse_send[0].astype(F32)
        columns_out[...] = stage[...].T

    degree, rows, _ = edges.shape
    part = own_part[pl.ds(pl.multiple_of(step * rows, rows), rows), :]
    product = matmul(edges[...].reshape(degree * rows, features), weights[...])
    pre_out[...] = product.reshape(degree, rows, features) + part[None]


def fine_kernel(
    nbr, pre, edges, nodes, own_table, siblings, core_rows, chip_rows, select,
    edge_in, edge_out, node_in, node_out,
    mid_out, core_out, chip_out, sums_out, share_out, meta_out,
    table, gathered, weight_out, weight_self, weight_sum, weight_last, mid_wide, meta,
):
    step = pl.program_id(0)
    steps = pl.num_programs(0)
    features = LANES
    degree, rows, _ = edges.shape
    halo = siblings.shape[1]
    own = own_table.shape[0]
    other = core_rows.shape[0] // 2
    even = is_even()

    @pl.when(step == 0)
    def _():
        weight_out[...] = square(centred(edge_out[...]))
        weight_self[...] = square(node_in[:features, :])
        weight_sum[...] = square(node_in[features:, :])
        weight_last[...] = square(centred(node_out[...]))
        to_table = square(edge_in[features : 2 * features, :])
        table[0:own, :] = own_table[...]
        table[own : own + 4 * halo, :] = matmul(
            siblings[...].reshape(4 * halo, features), to_table
        )
        core_at = pl.multiple_of(jnp.where(even, other, 0), 8)
        core_block = core_rows[pl.ds(core_at, other), :]
        chip_block = chip_rows[...]
        halo_at = own + 4 * halo
        core_to = pl.multiple_of(halo_at + jnp.where(even, halo, 0), 8)
        chip_to = pl.multiple_of(halo_at + jnp.where(even, 0, halo), 8)
        table[pl.ds(core_to, halo), :] = matmul(core_block[:halo], to_table)
        table[pl.ds(chip_to, halo), :] = matmul(chip_block[:halo], to_table)
        meta[...] = jnp.zeros_like(meta)
        meta[0:1, :] = core_block[halo : halo + 1] - 1.0
        meta[1:2, :] = chip_block[halo : halo + 1] - 1.0

    first = pl.multiple_of(step * rows, rows)

    def gather(group, carry):
        base = pl.multiple_of(group * 8, 8)
        for slot in range(degree):
            for offset in range(8):
                index = nbr[slot, first + base + offset]
                gathered[slot, pl.ds(base + offset, 1), :] = table[pl.ds(index, 1), :]
        return carry

    lax.fori_loop(0, rows // 8, gather, 0)
    hidden = jnp.maximum(pre[...] + gathered[...], 0.0).reshape(degree * rows, features)
    message = scaled(matmul(hidden, weight_out[...])).reshape(degree, rows, features)
    summed = jnp.sum(edges[...] + message, axis=0)
    own_rows = nodes[...]
    node_hidden = jnp.maximum(
        matmul(own_rows, weight_self[...]) + matmul(summed, weight_sum[...]), 0.0
    )
    mid = own_rows + scaled(matmul(node_hidden, weight_last[...]))
    mid_out[...] = mid
    mid_wide[pl.ds(first, rows), :] = wide(mid)

    @pl.when(step == steps - 1)
    def _():
        coarse = sums_out.shape[0]
        total = jnp.zeros((2 * coarse, 2 * LANES), F32)
        count = jnp.zeros((coarse, LANES), F32)
        places = iota((2 * coarse, LANES), 0)
        for block in range(select.shape[0]):
            place = jnp.where(places == select[block : block + 1, :], 1.0, 0.0)
            count = count + place[:coarse]
            total = total + jnp.dot(
                place.astype(BF16),
                mid_wide[block * LANES : (block + 1) * LANES, :],
                preferred_element_type=F32,
            )
        total = fold(total)
        sums_out[...] = total[:coarse]
        core_out[...] = total[coarse : coarse + LANES]
        chip_out[...] = total[coarse + LANES :]
        for source in range(2):
            count = count + jnp.where(places[:coarse] == meta[source : source + 1, :], 1.0, 0.0)
        members = jnp.maximum(jnp.sum(count, axis=1, keepdims=True), 1.0)
        share_out[...] = jnp.broadcast_to(1.0 / members, (coarse, LANES))
        meta_out[0:8, :] = meta[0:8, :]
        meta_out[8 : 8 + LANES, :] = meta[...].T


def pool_kernel(sums, share, meta, columns, core_rows, chip_rows, pooled_out, core_out, chip_out):
    coarse = sums.shape[0]
    even = is_even()
    other = core_rows.shape[0] // 2
    core_block = core_rows[pl.ds(pl.multiple_of(jnp.where(even, other, 0), 8), other), :]
    received = wide(jnp.concatenate([core_block, chip_rows[...]], axis=0))
    places = iota((coarse, LANES), 0)
    member = jnp.concatenate(
        [one_hot(places == meta[0:1, :]), one_hot(places == meta[1:2, :])], axis=1
    )
    pooled = (sums[...] + pick(member, received)) * share[...]
    pooled_out[...] = pooled
    pooled_wide = wide(pooled)
    rows = core_out.shape[0]
    lanes = iota((rows, coarse), 1)
    next_rows = pick(one_hot(lanes == columns[0:rows, 24:25]), pooled_wide)
    prev_rows = pick(one_hot(lanes == columns[0:rows, 25:26]), pooled_wide)
    core_out[...] = jnp.where(even, next_rows, prev_rows)
    chip_out[...] = jnp.where(even, prev_rows, next_rows)


def coarse_kernel(
    pooled_in, meta, columns, core_rows, chip_rows, edge_in, edge_out, node_in, node_out,
    refined_out, core_out, chip_out, table,
):
    features = LANES
    even = is_even()
    pooled = pooled_in[...]
    coarse = pooled.shape[0]
    other = core_rows.shape[0] // 2
    core_block = core_rows[pl.ds(pl.multiple_of(jnp.where(even, other, 0), 8), other), :]
    chip_block = chip_rows[...]
    to_table = square(edge_in[features:, :])
    prev_rows = jnp.where(even, chip_block, core_block)
    next_rows = jnp.where(even, core_block, chip_block)
    extended = jnp.concatenate([pooled, prev_rows, next_rows], axis=0)
    table[...] = wide(matmul(extended, to_table))
    from_own = matmul(pooled, square(edge_in[:features, :]))
    weight_out = square(centred(edge_out[...]))
    extent = extended.shape[0]
    lanes = iota((LANES, extent), 1)
    degree = 6
    summed = []
    for block in range(coarse // LANES):
        hot = jnp.concatenate(
            [
                one_hot(lanes == columns[:, 8 + 8 * block + slot : 9 + 8 * block + slot])
                for slot in range(degree)
            ],
            axis=0,
        )
        near = pick(hot, table[...]).reshape(degree, LANES, features)
        own = from_own[block * LANES : (block + 1) * LANES]
        hidden = jnp.maximum(near + own[None], 0.0).reshape(degree * LANES, features)
        message = scaled(matmul(hidden, weight_out)).reshape(degree, LANES, features)
        summed.append(jnp.sum(message, axis=0))
    total = jnp.concatenate(summed, axis=0)
    node_hidden = jnp.maximum(
        matmul(pooled, square(node_in[:features, :])) + matmul(total, square(node_in[features:, :])),
        0.0,
    )
    refined = pooled + scaled(matmul(node_hidden, square(centred(node_out[...]))))
    refined_out[...] = refined
    refined_wide = wide(refined)
    slots = iota((LANES, coarse), 1)
    core_out[...] = pick(one_hot(slots == meta[8 : 8 + LANES, 0:1]), refined_wide)
    chip_out[...] = pick(one_hot(slots == meta[8 : 8 + LANES, 1:2]), refined_wide)


def last_kernel(mid, refined, columns, core_rows, chip_rows, out, table):
    even = is_even()
    coarse = refined.shape[0]
    other = core_rows.shape[0] // 2
    core_block = core_rows[pl.ds(pl.multiple_of(jnp.where(even, other, 0), 8), other), :]
    table[0:coarse, :] = wide(refined[...])
    table[coarse : coarse + other, :] = wide(core_block)
    table[coarse + other :, :] = wide(chip_rows[...])
    lanes = iota((LANES, coarse + 2 * other), 1)
    for block in range(mid.shape[0] // LANES):
        rows = slice(block * LANES, (block + 1) * LANES)
        hot = one_hot(lanes == columns[:, block : block + 1])
        out[rows, :] = mid[rows, :] + pick(hot, table[...])


def shape(*dims):
    return jax.ShapeDtypeStruct(dims, F32)


def call(kernel, outs, args, places, scratch=(), grid=(), out_specs=None, flops=0, bytes_=0, vmem=None):
    whole = {"v": pl.BlockSpec(memory_space=VMEM), "s": pl.BlockSpec(memory_space=SMEM)}
    specs = [whole[p] if isinstance(p, str) else p for p in places]
    if out_specs is None:
        out_specs = [whole["v"]] * len(outs)
    return pl.pallas_call(
        kernel,
        out_shape=outs,
        grid=grid,
        in_specs=specs,
        out_specs=out_specs,
        scratch_shapes=list(scratch),
        cost_estimate=pl.CostEstimate(flops=flops, bytes_accessed=bytes_, transcendentals=0),
        compiler_params=pltpu.CompilerParams(vmem_limit_bytes=vmem or 32 * 2**20),
    )(*args)


def over_core(block):
    size = lax.axis_size("dom")
    groups = [[i, i + 1] for i in range(0, size, 2)]
    return lax.all_gather(block, "dom", axis=0, tiled=True, axis_index_groups=groups)


def over_chip(block):
    size = lax.axis_size("dom")
    route = []
    for i in range(1, size - 1, 2):
        route += [(i, i + 1), (i + 1, i)]
    return lax.ppermute(block, "dom", route)


def local(
    fine_nodes, fine_edges, fine_nbr, sub_send, dom_send, pool_owner, pool_slot, coarse_nbr,
    coarse_send, fine_edge_in, fine_edge_out, fine_node_in, fine_node_out, coarse_edge_in,
    coarse_edge_out, coarse_node_in, coarse_node_out,
):
    node_rows, features = fine_nodes.shape
    degree = fine_nbr.shape[0]
    coarse = coarse_nbr.shape[1]
    halo = sub_send.shape[2]
    coarse_halo = coarse_send.shape[2]
    capacity = node_rows // 8
    extent = node_rows + 6 * halo
    owner = pool_owner[:, 0].reshape(8, LANES)
    slot = pool_slot.reshape(8, LANES)

    sibling_send, core_send, chip_send, select = call(
        pack_kernel,
        [shape(4, halo, features), shape(halo + 8, features), shape(halo + 8, features), shape(8, LANES)],
        [sub_send, dom_send, owner, slot, fine_nodes],
        "ssvvv",
    )
    siblings = lax.all_to_all(sibling_send, "sub", 0, 0)
    chip_rows = over_chip(chip_send)
    core_rows = over_core(core_send)

    rows = LANES
    steps = node_rows // rows
    edge_block = pl.BlockSpec((degree, rows, features), lambda i: (0, i, 0))
    node_block = pl.BlockSpec((rows, features), lambda i: (i, 0))

    def fixed(*dims):
        return pl.BlockSpec(dims, lambda i: (0,) * len(dims))

    pre, own_table, columns = call(
        before_kernel,
        [shape(degree, node_rows, features), shape(node_rows, features), shape(LANES, LANES)],
        [fine_edges, fine_nodes, fine_edge_in, select, coarse_nbr, coarse_send],
        [
            edge_block, fixed(node_rows, features), fixed(3 * features, features),
            fixed(8, LANES), fixed(degree, coarse), fixed(1, 2, coarse_halo),
        ],
        scratch=[VMEM((256, 256), BF16), VMEM((node_rows, features), F32), VMEM((LANES, LANES), F32)],
        grid=(steps,),
        out_specs=[edge_block, fixed(node_rows, features), fixed(LANES, LANES)],
        flops=2 * 8192 * 128 * 128 * 6,
        bytes_=6291456,
    )
    weight = VMEM((256, 256), BF16)
    mid, core_send, chip_send, sums, share, meta = call(
        fine_kernel,
        [
            shape(node_rows, features), shape(capacity, features), shape(capacity, features),
            shape(coarse, features), shape(coarse, LANES), shape(8 + LANES, LANES),
        ],
        [
            fine_nbr, pre, fine_edges, fine_nodes, own_table, siblings, core_rows, chip_rows,
            select, fine_edge_in, fine_edge_out, fine_node_in, fine_node_out,
        ],
        [
            "s", edge_block, edge_block, node_block, fixed(node_rows, features),
            fixed(4, halo, features), fixed(2 * (halo + 8), features), fixed(halo + 8, features),
            fixed(8, LANES), fixed(3 * features, features), fixed(features, features),
            fixed(2 * features, features), fixed(features, features),
        ],
        scratch=[
            VMEM((extent, features), F32), VMEM((degree, rows, features), F32),
            weight, weight, weight, weight, VMEM((node_rows, 2 * LANES), BF16),
            VMEM((LANES, LANES), F32),
        ],
        grid=(steps,),
        out_specs=[
            node_block, fixed(capacity, features), fixed(capacity, features),
            fixed(coarse, features), fixed(coarse, LANES), fixed(8 + LANES, LANES),
        ],
        flops=2 * 8192 * 128 * 128 * 12,
        bytes_=8 * 2**20,
    )
    chip_rows = over_chip(chip_send)
    core_rows = over_core(core_send)
    pooled, core_send, chip_send = call(
        pool_kernel,
        [shape(coarse, features), shape(coarse_halo, features), shape(coarse_halo, features)],
        [sums, share, meta, columns, core_rows, chip_rows],
        "vvvvvv",
    )
    chip_rows = over_chip(chip_send)
    core_rows = over_core(core_send)
    refined, core_send, chip_send = call(
        coarse_kernel,
        [shape(coarse, features), shape(capacity, features), shape(capacity, features)],
        [
            pooled, meta, columns, core_rows, chip_rows,
            coarse_edge_in, coarse_edge_out, coarse_node_in, coarse_node_out,
        ],
        "vvvvvvvvv",
        scratch=[VMEM((coarse + 2 * coarse_halo, 2 * LANES), BF16)],
    )
    chip_rows = over_chip(chip_send)
    core_rows = over_core(core_send)
    (out,) = call(
        last_kernel,
        [shape(node_rows, features)],
        [mid, refined, columns, core_rows, chip_rows],
        "vvvvv",
        scratch=[VMEM((coarse + 2 * capacity, 2 * LANES), BF16)],
    )
    return out


def solution(mesh):
    rows = P(("dom", "sub"))
    slots = P(None, ("dom", "sub"))
    in_specs = (rows, slots, slots, rows, rows, rows, rows, slots, rows) + (P(),) * 8
    return jax.shard_map(local, mesh=mesh, in_specs=in_specs, out_specs=rows, check_vma=False)
```
